512 devices in a mesh: seq: 128 (over z, y, x_hi), batch: 4 (over x_lo, core).
Axes of the slice: x: 4 (x_hi: 2, x_lo: 2; x = x_hi * 2 + x_lo), y: 8, z: 8, core: 2. Of those that a mesh axis runs over, the one named last changes fastest.
Arguments:
- tokens: bfloat16 [4, 262144, 128], P('batch', 'seq'), may hold values from -6 to 6
- grad_out: bfloat16 [4, 262144, 128], P('batch', 'seq'), may hold values from -6 to 6
- kernel: bfloat16 [512, 512, 128], P(None, 'seq'), may hold values from -6 to 6
- mix_inner: bfloat16 [512, 512], replicated, may hold values from -0.25 to 0.25
- mix_outer: bfloat16 [512, 512], replicated, may hold values from -0.25 to 0.25
- unmix_outer: bfloat16 [512, 512], replicated, may hold values from -0.25 to 0.25
- unmix_inner: bfloat16 [512, 512], replicated, may hold values from -0.25 to 0.25
Outputs:
- output: bfloat16 [4, 262144, 128], P('batch', 'seq')
- grad_tokens: bfloat16 [4, 262144, 128], P('batch', 'seq')
- grad_kernel: float32 [512, 512, 128], P(None, 'seq', 'batch')
The draws below stay inside these ranges and needn't reach their ends.
All inputs are finite; a program needn't handle non-finite values.
Results may differ from the reference program's by a relative error of at most 0.018.
Values may be sent and summed in bfloat16 or wider, within the bound.
No kernel may reach another device: no remote copies, remote signals or barrier semaphores. Data moves between devices by JAX's collectives and lax.ppermute only.
A program may use at most 64 MiB of HBM per device.

```python
import jax
import jax.numpy as jnp
from jax import lax

BLK = 512
C = 128
LENGTH = 262144
BATCH = 4


def level_of(own_key, shape, split, low, top_value):
    loudness, own = 1.0, jax.random.fold_in(own_key, 6)
    for axis_at, blocks in split:
        draws = jnp.exp(jax.random.uniform(jax.random.fold_in(own, axis_at), (blocks,), jnp.float32, low / len(split), top_value / len(split)))
        loudness = loudness * jnp.repeat(draws, shape[axis_at] // blocks).reshape([-1 if axis == axis_at else 1 for axis in range(len(shape))])
    return loudness


def bell_draw(stream_key, shape, deviation, reach, cuts=(), kind=jnp.bfloat16):
    values = jax.random.normal(stream_key, shape, jnp.float32) * deviation
    if len(cuts) > 0:
        values = level_of(stream_key, shape, cuts, -0.22, 0.18) * values
    return jnp.clip(values, min=-reach, max=reach).astype(kind)


def setup_inputs(seed: int = 0) -> dict:
    keys = jax.random.split(jax.random.key(seed), 8)
    return {
        "tokens": bell_draw(keys[0], (BATCH, LENGTH, C), 1.0, 6.0, ((0, 4), (1, 128))),
        "grad_out": bell_draw(keys[1], (BATCH, LENGTH, C), 1.0, 6.0, ((0, 4), (1, 128))),
        "kernel": bell_draw(keys[2], (BLK, BLK, C), 1.0, 6.0, ((1, 128),)),
        "mix_inner": bell_draw(keys[3], (BLK, BLK), BLK ** -0.5, 0.25),
        "mix_outer": bell_draw(keys[4], (BLK, BLK), BLK ** -0.5, 0.25),
        "unmix_outer": bell_draw(keys[5], (BLK, BLK), BLK ** -0.5, 0.25),
        "unmix_inner": bell_draw(keys[6], (BLK, BLK), BLK ** -0.5, 0.25),
    }


def mm(pattern, left, right):
    return jnp.einsum(pattern, left.astype(jnp.float32), right.astype(jnp.float32)).astype(jnp.bfloat16)


def reference(tokens, grad_out, kernel, mix_inner, mix_outer, unmix_outer, unmix_inner):
    kernel_f = kernel.astype(jnp.float32)

    def single(carry, inputs):
        sample, target = inputs
        grid = sample.reshape(BLK, BLK, C)
        inner_mixed = mm("abc,bk->akc", grid, mix_inner)
        spectrum = mm("akc,am->mkc", inner_mixed, mix_outer)
        filtered = (kernel_f * spectrum.astype(jnp.float32)).astype(jnp.bfloat16)
        outer_done = mm("mkc,mn->nkc", filtered, unmix_outer)
        result = mm("nkc,kj->njc", outer_done, unmix_inner)
        cotangent = target.reshape(BLK, BLK, C)
        grad_inner = mm("njc,kj->nkc", cotangent, unmix_inner)
        grad_filtered = mm("nkc,mn->mkc", grad_inner, unmix_outer)
        term = spectrum.astype(jnp.float32) * grad_filtered.astype(jnp.float32)
        grad_spectrum = (kernel_f * grad_filtered.astype(jnp.float32)).astype(jnp.bfloat16)
        grad_outer = mm("mkc,am->akc", grad_spectrum, mix_outer)
        grad_tok = mm("akc,bk->abc", grad_outer, mix_inner)
        return carry + term, (result.reshape(LENGTH, C), grad_tok.reshape(LENGTH, C))

    start = jnp.zeros((BLK, BLK, C), jnp.float32)
    grad_kernel, stacked = lax.scan(single, start, (tokens, grad_out))
    return stacked[0], stacked[1], grad_kernel
```

```python
import jax
import jax.numpy as jnp
from jax import lax
from jax.sharding import PartitionSpec as P


def product(pattern, left, right):
    return jnp.einsum(pattern, left, right, preferred_element_type=jnp.float32).astype(jnp.bfloat16)


def batch_sum(terms):
    outer, inner, channels = terms.shape
    quarter = channels // 4
    place = lax.axis_index("batch")
    core, side = lax.rem(place, 2), lax.div(place, 2)
    parts = terms.reshape(outer, inner, 2, 2, quarter)
    mine = lax.dynamic_index_in_dim(parts, core, 3, keepdims=False)
    other = lax.dynamic_index_in_dim(parts, 1 - core, 3, keepdims=False).astype(jnp.bfloat16)
    got = lax.ppermute(other, "batch", [(0, 1), (1, 0), (2, 3), (3, 2)])
    pair = mine + got.astype(jnp.float32)
    keep = lax.dynamic_index_in_dim(pair, side, 2, keepdims=False)
    give = lax.dynamic_index_in_dim(pair, 1 - side, 2, keepdims=False).astype(jnp.bfloat16)
    got = lax.ppermute(give, "batch", [(0, 2), (2, 0), (1, 3), (3, 1)])
    return keep + got.astype(jnp.float32)


def body(tokens, grad_out, kernel, mix_inner, mix_outer, unmix_outer, unmix_inner):
    local_len, channels = tokens.shape[1:]
    block_len = mix_inner.shape[0]
    slab = local_len // block_len
    groups = block_len // slab
    tok_grid = tokens.reshape(slab, block_len, channels)
    cot_grid = grad_out.reshape(slab, block_len, channels)
    inner_mixed = product("abc,bk->kac", tok_grid, mix_inner)
    grad_inner = product("njc,kj->knc", cot_grid, unmix_inner)
    sent = jnp.stack(
        [inner_mixed.reshape(groups, slab * slab, channels), grad_inner.reshape(groups, slab * slab, channels)], axis=1
    ).reshape(groups, 2 * slab * slab, channels)
    here = lax.all_to_all(sent, "seq", split_axis=0, concat_axis=0, tiled=True)
    here = here.reshape(groups, 2, slab, slab, channels)
    spectrum = product("gkac,gam->mkc", here[:, 0], mix_outer.reshape(groups, slab, block_len))
    grad_filtered = product("gknc,mgn->mkc", here[:, 1], unmix_outer.reshape(block_len, groups, slab))
    kernel_f = kernel.astype(jnp.float32)
    spec_f = spectrum.astype(jnp.float32)
    gradf_f = grad_filtered.astype(jnp.float32)
    filtered = (kernel_f * spec_f).astype(jnp.bfloat16)
    grad_spectrum = (kernel_f * gradf_f).astype(jnp.bfloat16)
    outer_done = product("mkc,mn->nkc", filtered, unmix_outer)
    grad_outer = product("mkc,am->akc", grad_spectrum, mix_outer)
    sent = jnp.stack(
        [outer_done.reshape(groups, slab * slab, channels), grad_outer.reshape(groups, slab * slab, channels)], axis=1
    ).reshape(groups, 2 * slab * slab, channels)
    back = lax.all_to_all(sent, "seq", split_axis=0, concat_axis=0, tiled=True)
    grad_kernel = batch_sum(spec_f * gradf_f)
    back = back.reshape(groups, 2, slab, slab, channels)
    result = product("gnkc,gkj->njc", back[:, 0], unmix_inner.reshape(groups, slab, block_len))
    grad_tok = product("gakc,bgk->abc", back[:, 1], mix_inner.reshape(block_len, groups, slab))
    return (result.reshape(1, local_len, channels), grad_tok.reshape(1, local_len, channels), grad_kernel)


def solution(mesh):
    return jax.shard_map(
        body,
        mesh=mesh,
        in_specs=(
            P("batch", "seq", None),
            P("batch", "seq", None),
            P(None, "seq", None),
            P(),
            P(),
            P(),
            P(),
        ),
        out_specs=(P("batch", "seq", None), P("batch", "seq", None), P(None, "seq", "batch")),
        check_vma=False,
    )
```

```python
import functools

import jax
import jax.numpy as jnp
from jax import lax
from jax.experimental import pallas as pl
from jax.experimental.pallas import tpu as pltpu
from jax.sharding import PartitionSpec as P

VMEM_LIMIT = 24 * 1024 * 1024


def dot(left, right, left_dim=1):
    return lax.dot_general(left, right, (((left_dim,), (0,)), ((), ())), preferred_element_type=jnp.float32)


def scatter_rows(slab, product, scratch, out_ref, part):
    block, width = product.shape
    channels = width // slab
    for g in range(slab):
        scratch[pl.ds(g, block, stride=slab), :] = product[:, g * channels : (g + 1) * channels]
    rows = slab * slab
    out_ref[:, part * rows : (part + 1) * rows, :] = (
        scratch[...].astype(jnp.bfloat16).reshape(block // slab, rows, channels)
    )


def gather_rows(slab, groups, scratch, part):
    rows = slab * slab
    lanes = []
    for i in range(slab):
        pieces = [
            scratch[pl.ds(part * rows + i * slab + j, groups, stride=2 * rows), :].astype(jnp.bfloat16)
            for j in range(slab)
        ]
        lanes.append(jnp.concatenate(pieces, axis=0))
    return jnp.concatenate(lanes, axis=1)


def lanes_of(ref, slab):
    block = ref.shape[0] // slab
    return jnp.concatenate([ref[a * block : (a + 1) * block, :] for a in range(slab)], axis=1)


def before_kernel(slab, tok_ref, cot_ref, mix_ref, unmix_ref, out_ref, scratch):
    scatter_rows(slab, dot(mix_ref[...], lanes_of(tok_ref, slab), 0), scratch.at[0], out_ref, 0)
    scatter_rows(slab, dot(unmix_ref[...], lanes_of(cot_ref, slab)), scratch.at[1], out_ref, 1)


def between_kernel(slab, in_ref, ker_ref, mixt_ref, unmixp_ref, unmixt_ref, mix_ref, out_ref, term_ref, rows, scratch):
    groups = in_ref.shape[0]
    channels = in_ref.shape[2]
    rows[...] = in_ref[...].reshape(rows.shape).astype(jnp.float32)
    weight = ker_ref[...].astype(jnp.float32)
    spectrum = dot(mixt_ref[...], gather_rows(slab, groups, rows, 0)).astype(jnp.bfloat16).astype(jnp.float32)
    filtered = (weight * spectrum).astype(jnp.bfloat16)
    scatter_rows(slab, dot(unmixt_ref[...], filtered), scratch.at[0], out_ref, 0)
    gradf = dot(unmixp_ref[...], gather_rows(slab, groups, rows, 1)).astype(jnp.bfloat16).astype(jnp.float32)
    grad_spectrum = (weight * gradf).astype(jnp.bfloat16)
    scatter_rows(slab, dot(mix_ref[...], grad_spectrum), scratch.at[1], out_ref, 1)
    terms = spectrum * gradf
    for i in range(slab):
        term_ref[i] = terms[:, i * channels : (i + 1) * channels]


def after_kernel(slab, in_ref, unmixt_ref, mixp_ref, res_ref, tok_ref, rows):
    groups = in_ref.shape[0]
    channels = in_ref.shape[2]
    block = unmixt_ref.shape[0]
    rows[...] = in_ref[...].reshape(rows.shape).astype(jnp.float32)
    for part, (weight_ref, out_ref) in enumerate(((unmixt_ref, res_ref), (mixp_ref, tok_ref))):
        product = dot(weight_ref[...], gather_rows(slab, groups, rows, part)).astype(jnp.bfloat16)
        for i in range(slab):
            out_ref[i * block : (i + 1) * block, :] = product[:, i * channels : (i + 1) * channels]


def call(kernel, outs, scratch, *args):
    return pl.pallas_call(
        kernel,
        out_shape=outs,
        in_specs=[pl.BlockSpec(memory_space=pltpu.VMEM)] * len(args),
        out_specs=jax.tree.map(lambda _: pl.BlockSpec(memory_space=pltpu.VMEM), outs),
        scratch_shapes=scratch,
        compiler_params=pltpu.CompilerParams(vmem_limit_bytes=VMEM_LIMIT),
    )(*args)


def batch_sum(terms):
    inner, outer, channels = terms.shape
    quarter = channels // 4
    place = lax.axis_index("batch")
    core, side = lax.rem(place, 2), lax.div(place, 2)
    parts = terms.reshape(inner, outer, 2, 2, quarter)
    mine = lax.dynamic_index_in_dim(parts, core, 3, keepdims=False)
    other = lax.dynamic_index_in_dim(parts, 1 - core, 3, keepdims=False).astype(jnp.bfloat16)
    got = lax.ppermute(other, "batch", [(0, 1), (1, 0), (2, 3), (3, 2)])
    pair = mine + got.astype(jnp.float32)
    keep = lax.dynamic_index_in_dim(pair, side, 2, keepdims=False)
    give = lax.dynamic_index_in_dim(pair, 1 - side, 2, keepdims=False).astype(jnp.bfloat16)
    got = lax.ppermute(give, "batch", [(0, 2), (2, 0), (1, 3), (3, 1)])
    return (keep + got.astype(jnp.float32)).transpose(1, 0, 2)


def body(tokens, grad_out, kernel, mix_inner, mix_outer, unmix_outer, unmix_inner):
    local_len, channels = tokens.shape[1:]
    block = mix_inner.shape[0]
    slab = local_len // block
    groups = block // slab
    bf16, f32 = jnp.bfloat16, jnp.float32
    message = jax.ShapeDtypeStruct((groups, 2 * slab * slab, channels), bf16)
    stage = pltpu.VMEM((2, block * slab, channels), f32)
    rows = pltpu.VMEM((2 * block * slab, channels), f32)

    def columns(weight):
        return weight.reshape(block, groups, slab).transpose(0, 2, 1).reshape(block, block)

    sent = call(
        functools.partial(before_kernel, slab),
        message,
        [stage],
        tokens.reshape(local_len, channels),
        grad_out.reshape(local_len, channels),
        mix_inner,
        unmix_inner,
    )
    here = lax.all_to_all(sent, "seq", split_axis=0, concat_axis=0, tiled=True)
    sent, terms = call(
        functools.partial(between_kernel, slab),
        (message, jax.ShapeDtypeStruct((slab, block, channels), f32)),
        [rows, stage],
        here,
        kernel.reshape(block, slab * channels),
        columns(mix_outer.T),
        columns(unmix_outer),
        unmix_outer.T,
        mix_outer,
    )
    back = lax.all_to_all(sent, "seq", split_axis=0, concat_axis=0, tiled=True)
    grad_kernel = batch_sum(terms)
    flat = jax.ShapeDtypeStruct((local_len, channels), bf16)
    output, grad_tokens = call(
        functools.partial(after_kernel, slab),
        (flat, flat),
        [rows],
        back,
        columns(unmix_inner.T),
        columns(mix_inner),
    )
    return (output.reshape(1, local_len, channels), grad_tokens.reshape(1, local_len, channels), grad_kernel)


def solution(mesh):
    return jax.shard_map(
        body,
        mesh=mesh,
        in_specs=(
            P("batch", "seq", None),
            P("batch", "seq", None),
            P(None, "seq", None),
            P(),
            P(),
            P(),
            P(),
        ),
        out_specs=(P("batch", "seq", None), P("batch", "seq", None), P(None, "seq", "batch")),
        check_vma=False,
    )
```

```python
import functools

import jax
import jax.numpy as jnp
from jax import lax
from jax.experimental import pallas as pl
from jax.experimental.pallas import tpu as pltpu
from jax.sharding import PartitionSpec as P

SUBLANES = 8
WHOLE_VMEM = 62 * 1024 * 1024
MOST_VMEM = 24 * 1024 * 1024


def dot(left, right, left_dim=1):
    return lax.dot_general(left, right, (((left_dim,), (0,)), ((), ())), preferred_element_type=jnp.float32)


class Copies:
    def __init__(self, sems):
        self.sems, self.started = sems, []

    def start(self, src, dst):
        copy = pltpu.make_async_copy(src, dst, self.sems.at[len(self.started)])
        copy.start()
        self.started.append(copy)
        return copy


def scatter_rows(slab, product, stage, out_buf, part):
    block, width = product.shape
    channels = width // slab
    for g in range(slab):
        stage[pl.ds(g, block, stride=slab), :] = product[:, g * channels : (g + 1) * channels]
    rows = slab * slab
    out_buf[:, part * rows : (part + 1) * rows, :] = (
        stage[...].astype(jnp.bfloat16).reshape(block // slab, rows, channels)
    )


def gather_rows(slab, in_ref, part):
    groups, _, channels = in_ref.shape
    rows = slab * slab
    tiles = rows // SUBLANES
    got = in_ref[:, part * rows : (part + 1) * rows, :].astype(jnp.float32)
    got = got.reshape(groups // 2, 2, tiles, SUBLANES, channels)
    turned = pltpu.roll(got.reshape(groups * tiles, SUBLANES, channels), slab, axis=1).reshape(got.shape)
    low = lax.broadcasted_iota(jnp.int32, (groups // 2, tiles, SUBLANES, channels), 2) < slab
    even = jnp.where(low, got[:, 0], turned[:, 1]).astype(jnp.bfloat16)
    odd = jnp.where(low, turned[:, 0], got[:, 1]).astype(jnp.bfloat16)
    lanes = [half[:, t].reshape(groups * slab, channels) for t in range(tiles) for half in (even, odd)]
    return jnp.concatenate(lanes, axis=1)


def lanes_of(ref, slab):
    block = ref.shape[0] // slab
    return jnp.concatenate([ref[a * block : (a + 1) * block, :] for a in range(slab)], axis=1)


def part_of(ref, rows, part):
    return ref.at[:, pl.ds(part * rows, rows)]


def far_of(weights, shape):
    block, channels = weights[0].shape[0], shape[2]
    rows = [weight.reshape(block, block // channels, channels).transpose(1, 0, 2) for weight in weights]
    return jnp.concatenate(rows, axis=0).reshape(shape)


def near_of(far, block):
    parts = block // far.shape[2]
    step = far.shape[0] // parts
    return jnp.concatenate([far[t * step : (t + 1) * step].reshape(block, far.shape[2]) for t in range(parts)], axis=1)


def before_kernel(slab, tok_hbm, cot_hbm, mix_hbm, unmix_hbm, out_ref, tok, cot, mix, unmix, stage, out_buf, sems):
    copies = Copies(sems)
    got = [copies.start(src, dst) for src, dst in ((mix_hbm, mix), (tok_hbm, tok), (unmix_hbm, unmix), (cot_hbm, cot))]
    rows = slab * slab
    given = []
    for part, (weight, data, left_dim) in enumerate(((mix, tok, 0), (unmix, cot, 1))):
        got[2 * part].wait()
        got[2 * part + 1].wait()
        scatter_rows(slab, dot(weight[...], lanes_of(data, slab), left_dim), stage.at[part], out_buf, part)
        given.append(copies.start(part_of(out_buf, rows, part), part_of(out_ref, rows, part)))
    for copy in given:
        copy.wait()


def between_kernel(
    slab, in_hbm, ker_hbm, far_hbm, out_ref, term_ref, in_ref, ker, mix_rows, unmix_rows, stage, out_buf, term_buf, sems
):
    channels = in_ref.shape[2]
    block = ker.shape[1]
    rows = slab * slab
    copies = Copies(sems)
    got_in = copies.start(in_hbm, in_ref)
    half = mix_rows.shape[0]
    got_mix = copies.start(far_hbm.at[pl.ds(0, half)], mix_rows)
    got_unmix = copies.start(far_hbm.at[pl.ds(half, half)], unmix_rows)
    got_ker = copies.start(ker_hbm, ker)
    got_in.wait()
    mixed = gather_rows(slab, in_ref, 0)
    cotangent = gather_rows(slab, in_ref, 1)
    got_mix.wait()
    mix = near_of(mix_rows, block)
    spectrum = dot(mix, mixed, 0).astype(jnp.bfloat16).astype(jnp.float32)
    got_unmix.wait()
    unmix = near_of(unmix_rows, block)
    gradf = dot(unmix, cotangent).astype(jnp.bfloat16).astype(jnp.float32)
    terms = spectrum * gradf
    got_ker.wait()
    for i in range(slab):
        term_buf[i] = terms[:, i * channels : (i + 1) * channels]
    given = [copies.start(term_buf, term_ref)]
    weight = jnp.concatenate([ker[i] for i in range(slab)], axis=1)
    filtered = (weight * spectrum).astype(jnp.bfloat16)
    scatter_rows(slab, dot(unmix, filtered, 0), stage.at[0], out_buf, 0)
    given.append(copies.start(part_of(out_buf, rows, 0), part_of(out_ref, rows, 0)))
    grad_spectrum = (weight * gradf).astype(jnp.bfloat16)
    scatter_rows(slab, dot(mix, grad_spectrum), stage.at[1], out_buf, 1)
    given.append(copies.start(part_of(out_buf, rows, 1), part_of(out_ref, rows, 1)))
    for copy in given:
        copy.wait()


def after_kernel(slab, in_hbm, unmix_hbm, mix_hbm, res_ref, tok_ref, in_ref, unmix, mix, out_buf, sems):
    channels = in_ref.shape[2]
    block = unmix.shape[0]
    copies = Copies(sems)
    got_in = copies.start(in_hbm, in_ref)
    got = [copies.start(unmix_hbm, unmix), copies.start(mix_hbm, mix)]
    got_in.wait()
    arrived = [gather_rows(slab, in_ref, part) for part in range(2)]
    given = []
    for part, (weight, left_dim, out_ref) in enumerate(((unmix, 0, res_ref), (mix, 1, tok_ref))):
        got[part].wait()
        product = dot(weight[...], arrived[part], left_dim).astype(jnp.bfloat16)
        for i in range(slab):
            out_buf[part, i * block : (i + 1) * block, :] = product[:, i * channels : (i + 1) * channels]
        given.append(copies.start(out_buf.at[part], out_ref))
    for copy in given:
        copy.wait()


def call(kernel, outs, specs, scratch, copies, limit, flops, aliases, *args):
    return pl.pallas_call(
        kernel,
        out_shape=outs,
        in_specs=[pl.BlockSpec(memory_space=space) for space in specs],
        out_specs=jax.tree.map(lambda _: pl.BlockSpec(memory_space=pl.ANY), outs),
        scratch_shapes=[*scratch, pltpu.SemaphoreType.DMA((copies,))],
        input_output_aliases=aliases,
        compiler_params=pltpu.CompilerParams(vmem_limit_bytes=limit),
        cost_estimate=pl.CostEstimate(flops=flops, bytes_accessed=4 * 1024 * 1024, transcendentals=0),
    )(*args)


def kernels(block, slab, channels):
    local_len, groups = block * slab, block // slab
    bf16, f32 = jnp.bfloat16, jnp.float32
    ANY, VMEM = pl.ANY, pltpu.VMEM
    message = jax.ShapeDtypeStruct((groups, 2 * slab * slab, channels), bf16)
    flat = jax.ShapeDtypeStruct((local_len, channels), bf16)
    stage = VMEM((2, local_len, channels), f32)
    buffer = VMEM(message.shape, bf16)
    piece, matrix = VMEM((local_len, channels), bf16), VMEM((block, block), bf16)
    flops = 2 * block * block * slab * channels
    before = functools.partial(
        call, functools.partial(before_kernel, slab), message, [ANY] * 4,
        [piece, piece, matrix, matrix, stage, buffer], 6, WHOLE_VMEM, 2 * flops, {},
    )
    between = functools.partial(
        call, functools.partial(between_kernel, slab), (message, jax.ShapeDtypeStruct((slab, block, channels), f32)),
        [ANY] * 3,
        [buffer, VMEM((slab, block, channels), f32)] + [VMEM((groups // 2, 2 * slab * slab, channels), bf16)] * 2
        + [stage, buffer, VMEM((slab, block, channels), f32)], 7, MOST_VMEM, 4 * flops, {1: 1, 2: 0},
    )
    after = functools.partial(
        call, functools.partial(after_kernel, slab), (flat, flat), [ANY] * 3,
        [buffer, matrix, matrix, VMEM((2, local_len, channels), bf16)], 5, MOST_VMEM, 2 * flops, {},
    )
    return before, between, after


def batch_sum(terms):
    inner, outer, channels = terms.shape
    quarter = channels // 4
    place = lax.axis_index("batch")
    core, side = lax.rem(place, 2), lax.div(place, 2)
    parts = terms.reshape(inner, outer, 2, 2, quarter)
    mine = lax.dynamic_index_in_dim(parts, core, 3, keepdims=False)
    other = lax.dynamic_index_in_dim(parts, 1 - core, 3, keepdims=False).astype(jnp.bfloat16)
    got = lax.ppermute(other, "batch", [(0, 1), (1, 0), (2, 3), (3, 2)])
    pair = mine + got.astype(jnp.float32)
    keep = lax.dynamic_index_in_dim(pair, side, 2, keepdims=False)
    give = lax.dynamic_index_in_dim(pair, 1 - side, 2, keepdims=False).astype(jnp.bfloat16)
    got = lax.ppermute(give, "batch", [(0, 2), (2, 0), (1, 3), (3, 1)])
    return (keep + got.astype(jnp.float32)).transpose(1, 0, 2)


def body(tokens, grad_out, kernel, mix_inner, mix_outer, unmix_outer, unmix_inner):
    local_len, channels = tokens.shape[1:]
    block = mix_inner.shape[0]
    slab = local_len // block
    before, between, after = kernels(block, slab, channels)
    sent = before(tokens.reshape(local_len, channels), grad_out.reshape(local_len, channels), mix_inner, unmix_inner)
    here = lax.all_to_all(sent, "seq", split_axis=0, concat_axis=0, tiled=True)
    far = far_of((mix_outer, unmix_outer), (block // slab, 2 * slab * slab, channels))
    sent, terms = between(here, kernel.transpose(1, 0, 2).astype(jnp.float32), far)
    back = lax.all_to_all(sent, "seq", split_axis=0, concat_axis=0, tiled=True)
    grad_kernel = batch_sum(terms)
    output, grad_tokens = after(back, unmix_inner, mix_inner)
    return (output.reshape(1, local_len, channels), grad_tokens.reshape(1, local_len, channels), grad_kernel)


def solution(mesh):
    return jax.shard_map(
        body,
        mesh=mesh,
        in_specs=(
            P("batch", "seq", None),
            P("batch", "seq", None),
            P(None, "seq", None),
            P(),
            P(),
            P(),
            P(),
        ),
        out_specs=(P("batch", "seq", None), P("batch", "seq", None), P(None, "seq", "batch")),
        check_vma=False,
    )
```

```python
import functools

import jax
import jax.numpy as jnp
from jax import lax
from jax.experimental import pallas as pl
from jax.experimental.pallas import tpu as pltpu
from jax.sharding import PartitionSpec as P

SUBLANES = 8
WHOLE_VMEM = 62 * 1024 * 1024
MOST_VMEM = 24 * 1024 * 1024


def dot(left, right, left_dim=1):
    return lax.dot_general(left, right, (((left_dim,), (0,)), ((), ())), preferred_element_type=jnp.float32)


class Copies:
    def __init__(self, sems):
        self.sems, self.started = sems, []

    def start(self, src, dst):
        copy = pltpu.make_async_copy(src, dst, self.sems.at[len(self.started)])
        copy.start()
        self.started.append(copy)
        return copy


def scatter_rows(slab, product, stage, out_buf, part):
    block, width = product.shape
    channels = width // slab
    for g in range(slab):
        stage[pl.ds(g, block, stride=slab), :] = product[:, g * channels : (g + 1) * channels]
    rows = slab * slab
    out_buf[:, part * rows : (part + 1) * rows, :] = (
        stage[...].astype(jnp.bfloat16).reshape(block // slab, rows, channels)
    )


def gather_rows(slab, in_ref, part):
    groups, _, channels = in_ref.shape
    rows = slab * slab
    tiles = rows // SUBLANES
    got = in_ref[:, part * rows : (part + 1) * rows, :].astype(jnp.float32)
    got = got.reshape(groups // 2, 2, tiles, SUBLANES, channels)
    turned = pltpu.roll(got.reshape(groups * tiles, SUBLANES, channels), slab, axis=1).reshape(got.shape)
    low = lax.broadcasted_iota(jnp.int32, (groups // 2, tiles, SUBLANES, channels), 2) < slab
    even = jnp.where(low, got[:, 0], turned[:, 1]).astype(jnp.bfloat16)
    odd = jnp.where(low, turned[:, 0], got[:, 1]).astype(jnp.bfloat16)
    lanes = [half[:, t].reshape(groups * slab, channels) for t in range(tiles) for half in (even, odd)]
    return jnp.concatenate(lanes, axis=1)


def lanes_of(ref, slab):
    block = ref.shape[0] // slab
    return jnp.concatenate([ref[a * block : (a + 1) * block, :] for a in range(slab)], axis=1)


def part_of(ref, rows, part):
    return ref.at[:, pl.ds(part * rows, rows)]


def far_of(kernel, shape):
    rows = kernel.transpose(1, 0, 2).reshape(-1, shape[1], shape[2])
    return jnp.concatenate([rows] * (shape[0] // rows.shape[0]), axis=0)


def near_of(far, block):
    parts = block // far.shape[2]
    step = far.shape[0] // parts
    return jnp.concatenate([far[t * step : (t + 1) * step].reshape(block, far.shape[2]) for t in range(parts)], axis=1)


def before_kernel(slab, tok_hbm, cot_hbm, mix_hbm, unmix_hbm, out_ref, tok, cot, mix, unmix, stage, out_buf, sems):
    copies = Copies(sems)
    got = [copies.start(src, dst) for src, dst in ((mix_hbm, mix), (tok_hbm, tok), (unmix_hbm, unmix), (cot_hbm, cot))]
    rows = slab * slab
    given = []
    for part, (weight, data, left_dim) in enumerate(((mix, tok, 0), (unmix, cot, 1))):
        got[2 * part].wait()
        got[2 * part + 1].wait()
        scatter_rows(slab, dot(weight[...], lanes_of(data, slab), left_dim), stage.at[part], out_buf, part)
        given.append(copies.start(part_of(out_buf, rows, part), part_of(out_ref, rows, part)))
    for copy in given:
        copy.wait()


def between_kernel(slab, in_ref, mix, unmix, far_hbm, out_ref, term_ref, ker_rows, stage, out_buf, term_buf, sems):
    block, channels = mix.shape[0], in_ref.shape[2]
    rows = slab * slab
    copies = Copies(sems)
    got_ker = copies.start(far_hbm.at[pl.ds(0, ker_rows.shape[0])], ker_rows)
    spectrum = dot(mix[...], gather_rows(slab, in_ref, 0), 0).astype(jnp.bfloat16).astype(jnp.float32)
    gradf = dot(unmix[...], gather_rows(slab, in_ref, 1)).astype(jnp.bfloat16).astype(jnp.float32)
    terms = spectrum * gradf
    for i in range(slab):
        term_buf[i] = terms[:, i * channels : (i + 1) * channels]
    got_ker.wait()
    given = [copies.start(term_buf, term_ref)]
    weight = near_of(ker_rows, block).astype(jnp.float32)
    filtered = (weight * spectrum).astype(jnp.bfloat16)
    scatter_rows(slab, dot(unmix[...], filtered, 0), stage.at[0], out_buf, 0)
    given.append(copies.start(part_of(out_buf, rows, 0), part_of(out_ref, rows, 0)))
    grad_spectrum = (weight * gradf).astype(jnp.bfloat16)
    scatter_rows(slab, dot(mix[...], grad_spectrum), stage.at[1], out_buf, 1)
    given.append(copies.start(part_of(out_buf, rows, 1), part_of(out_ref, rows, 1)))
    for copy in given:
        copy.wait()


def after_kernel(slab, in_ref, unmix, mix, res_ref, tok_ref, out_buf, sems):
    channels = in_ref.shape[2]
    block = unmix.shape[0]
    copies = Copies(sems)
    given = []
    for part, (weight, left_dim, out_ref) in enumerate(((unmix, 0, res_ref), (mix, 1, tok_ref))):
        product = dot(weight[...], gather_rows(slab, in_ref, part), left_dim).astype(jnp.bfloat16)
        for i in range(slab):
            out_buf[part, i * block : (i + 1) * block, :] = product[:, i * channels : (i + 1) * channels]
        given.append(copies.start(out_buf.at[part], out_ref))
    for copy in given:
        copy.wait()


def call(kernel, outs, specs, scratch, copies, limit, flops, aliases, *args):
    return pl.pallas_call(
        kernel,
        out_shape=outs,
        in_specs=[pl.BlockSpec(memory_space=space) for space in specs],
        out_specs=jax.tree.map(lambda _: pl.BlockSpec(memory_space=pl.ANY), outs),
        scratch_shapes=[*scratch, pltpu.SemaphoreType.DMA((copies,))],
        input_output_aliases=aliases,
        compiler_params=pltpu.CompilerParams(vmem_limit_bytes=limit),
        cost_estimate=pl.CostEstimate(flops=flops, bytes_accessed=4 * 1024 * 1024, transcendentals=0),
    )(*args)


def kernels(block, slab, channels):
    local_len, groups = block * slab, block // slab
    bf16, f32 = jnp.bfloat16, jnp.float32
    ANY, VMEM = pl.ANY, pltpu.VMEM
    message = jax.ShapeDtypeStruct((groups, 2 * slab * slab, channels), bf16)
    flat = jax.ShapeDtypeStruct((local_len, channels), bf16)
    stage = VMEM((2, local_len, channels), f32)
    buffer = VMEM(message.shape, bf16)
    piece, matrix = VMEM((local_len, channels), bf16), VMEM((block, block), bf16)
    flops = 2 * block * block * slab * channels
    before = functools.partial(
        call, functools.partial(before_kernel, slab), message, [ANY] * 4,
        [piece, piece, matrix, matrix, stage, buffer], 6, WHOLE_VMEM, 2 * flops, {},
    )
    between = functools.partial(
        call, functools.partial(between_kernel, slab), (message, jax.ShapeDtypeStruct((slab, block, channels), f32)),
        [VMEM, VMEM, VMEM, ANY],
        [VMEM((groups // 2, *message.shape[1:]), bf16), stage, buffer, VMEM((slab, block, channels), f32)],
        4, MOST_VMEM, 4 * flops, {3: 0},
    )
    after = functools.partial(
        call, functools.partial(after_kernel, slab), (flat, flat), [VMEM] * 3,
        [VMEM((2, local_len, channels), bf16)], 2, MOST_VMEM, 2 * flops, {},
    )
    return before, between, after


def batch_sum(terms):
    inner, outer, channels = terms.shape
    quarter = channels // 4
    place = lax.axis_index("batch")
    core, side = lax.rem(place, 2), lax.div(place, 2)
    parts = terms.reshape(inner, outer, 2, 2, quarter)
    mine = lax.dynamic_index_in_dim(parts, core, 3, keepdims=False)
    other = lax.dynamic_index_in_dim(parts, 1 - core, 3, keepdims=False).astype(jnp.bfloat16)
    got = lax.ppermute(other, "batch", [(0, 1), (1, 0), (2, 3), (3, 2)])
    pair = mine + got.astype(jnp.float32)
    keep = lax.dynamic_index_in_dim(pair, side, 2, keepdims=False)
    give = lax.dynamic_index_in_dim(pair, 1 - side, 2, keepdims=False).astype(jnp.bfloat16)
    got = lax.ppermute(give, "batch", [(0, 2), (2, 0), (1, 3), (3, 1)])
    return (keep + got.astype(jnp.float32)).transpose(1, 0, 2)


def body(tokens, grad_out, kernel, mix_inner, mix_outer, unmix_outer, unmix_inner):
    local_len, channels = tokens.shape[1:]
    block = mix_inner.shape[0]
    slab = local_len // block
    before, between, after = kernels(block, slab, channels)
    sent = before(tokens.reshape(local_len, channels), grad_out.reshape(local_len, channels), mix_inner, unmix_inner)
    here = lax.all_to_all(sent, "seq", split_axis=0, concat_axis=0, tiled=True)
    far = far_of(kernel, (block // slab, 2 * slab * slab, channels))
    sent, terms = between(here, mix_outer, unmix_outer, far)
    back = lax.all_to_all(sent, "seq", split_axis=0, concat_axis=0, tiled=True)
    grad_kernel = batch_sum(terms)
    output, grad_tokens = after(back, unmix_inner, mix_inner)
    return (output.reshape(1, local_len, channels), grad_tokens.reshape(1, local_len, channels), grad_kernel)


def solution(mesh):
    return jax.shard_map(
        body,
        mesh=mesh,
        in_specs=(
            P("batch", "seq", None),
            P("batch", "seq", None),
            P(None, "seq", None),
            P(),
            P(),
            P(),
            P(),
        ),
        out_specs=(P("batch", "seq", None), P("batch", "seq", None), P(None, "seq", "batch")),
        check_vma=False,
    )
```

```python
import functools

import jax
import jax.numpy as jnp
from jax import lax
from jax.experimental import pallas as pl
from jax.experimental.pallas import tpu as pltpu
from jax.sharding import PartitionSpec as P

SUBLANES = 8
HALVES = 2
WHOLE_VMEM = 62 * 1024 * 1024
MOST_VMEM = 24 * 1024 * 1024


def dot(left, right, left_dim=1):
    return lax.dot_general(left, right, (((left_dim,), (0,)), ((), ())), preferred_element_type=jnp.float32)


class Copies:
    def __init__(self, sems):
        self.sems, self.started = sems, []

    def start(self, src, dst):
        copy = pltpu.make_async_copy(src, dst, self.sems.at[len(self.started)])
        copy.start()
        self.started.append(copy)
        return copy


def halves(block):
    return [slice(h * (block // HALVES), (h + 1) * (block // HALVES)) for h in range(HALVES)]


def rows_of(weight, left_dim, cut):
    return weight[:, cut] if left_dim == 0 else weight[cut, :]


def send_product(slab, weight, left_dim, right, stage, out_buf, out_ref, part, copies):
    block, width = right.shape
    channels = width // slab
    rows = slab * slab
    here = pl.ds(part * rows, rows)
    given = []
    for cut in halves(block):
        product = dot(rows_of(weight, left_dim, cut), right, left_dim)
        height = cut.stop - cut.start
        for g in range(slab):
            stage[pl.ds(cut.start * slab + g, height, stride=slab), :] = product[:, g * channels : (g + 1) * channels]
        groups = pl.ds(cut.start // slab, height // slab)
        ready = stage[pl.ds(cut.start * slab, height * slab), :].astype(jnp.bfloat16)
        out_buf[groups, here, :] = ready.reshape(height // slab, rows, channels)
        given.append(copies.start(out_buf.at[groups, here], out_ref.at[groups, here]))
    return given


def gather_rows(slab, in_ref, part):
    groups, _, channels = in_ref.shape
    rows = slab * slab
    tiles = rows // SUBLANES
    got = in_ref[:, part * rows : (part + 1) * rows, :].astype(jnp.float32)
    got = got.reshape(groups // 2, 2, tiles, SUBLANES, channels)
    turned = pltpu.roll(got.reshape(groups * tiles, SUBLANES, channels), slab, axis=1).reshape(got.shape)
    low = lax.broadcasted_iota(jnp.int32, (groups // 2, tiles, SUBLANES, channels), 2) < slab
    even = jnp.where(low, got[:, 0], turned[:, 1]).astype(jnp.bfloat16)
    odd = jnp.where(low, turned[:, 0], got[:, 1]).astype(jnp.bfloat16)
    lanes = [half[:, t].reshape(groups * slab, channels) for t in range(tiles) for half in (even, odd)]
    return jnp.concatenate(lanes, axis=1)


def lanes_of(ref, slab):
    block = ref.shape[0] // slab
    return jnp.concatenate([ref[a * block : (a + 1) * block, :] for a in range(slab)], axis=1)


def before_kernel(slab, tok_hbm, cot_hbm, mix_hbm, unmix_hbm, out_ref, tok, cot, mix, unmix, stage, out_buf, sems):
    copies = Copies(sems)
    got = [copies.start(src, dst) for src, dst in ((mix_hbm, mix), (tok_hbm, tok), (unmix_hbm, unmix), (cot_hbm, cot))]
    given = []
    for part, (weight, data, left_dim) in enumerate(((mix, tok, 0), (unmix, cot, 1))):
        got[2 * part].wait()
        got[2 * part + 1].wait()
        given += send_product(slab, weight, left_dim, lanes_of(data, slab), stage.at[part], out_buf, out_ref, part, copies)
    for copy in given:
        copy.wait()


def between_kernel(slab, in_ref, mix, unmix, ker_hbm, out_ref, term_ref, ker, ker_rows, stage, out_buf, sems):
    block, channels = mix.shape[0], in_ref.shape[2]
    copies = Copies(sems)
    got_ker = copies.start(ker_hbm, ker)
    spectrum = dot(mix[...], gather_rows(slab, in_ref, 0), 0).astype(jnp.bfloat16).astype(jnp.float32)
    gradf = dot(unmix[...], gather_rows(slab, in_ref, 1)).astype(jnp.bfloat16).astype(jnp.float32)
    got_ker.wait()
    ker_rows[...] = ker[...].astype(jnp.float32)
    weight = jnp.concatenate([ker_rows[pl.ds(i, block, stride=slab), :] for i in range(slab)], axis=1)
    filtered = (weight * spectrum).astype(jnp.bfloat16)
    given = send_product(slab, unmix, 0, filtered, stage.at[0], out_buf, out_ref, 0, copies)
    grad_spectrum = (weight * gradf).astype(jnp.bfloat16)
    given += send_product(slab, mix, 1, grad_spectrum, stage.at[1], out_buf, out_ref, 1, copies)
    terms = spectrum * gradf
    for i in range(slab):
        term_ref[i] = terms[:, i * channels : (i + 1) * channels]
    for copy in given:
        copy.wait()


def after_kernel(slab, in_ref, unmix, mix, res_ref, tok_ref, out_buf, sems):
    channels = in_ref.shape[2]
    block = unmix.shape[0]
    copies = Copies(sems)
    given = []
    for part, (weight, left_dim, out_ref) in enumerate(((unmix, 0, res_ref), (mix, 1, tok_ref))):
        arrived = gather_rows(slab, in_ref, part)
        for cut in halves(block):
            product = dot(rows_of(weight, left_dim, cut), arrived, left_dim).astype(jnp.bfloat16)
            here = pl.ds(cut.start, cut.stop - cut.start)
            for i in range(slab):
                out_buf[part, i, here, :] = product[:, i * channels : (i + 1) * channels]
            given.append(copies.start(out_buf.at[part, :, here], out_ref.at[:, here]))
    for copy in given:
        copy.wait()


def call(kernel, outs, out_specs, specs, scratch, copies, limit, flops, aliases, *args):
    return pl.pallas_call(
        kernel,
        out_shape=outs,
        in_specs=[pl.BlockSpec(memory_space=space) for space in specs],
        out_specs=jax.tree.map(lambda space: pl.BlockSpec(memory_space=space), out_specs),
        scratch_shapes=[*scratch, pltpu.SemaphoreType.DMA((copies,))],
        input_output_aliases=aliases,
        compiler_params=pltpu.CompilerParams(vmem_limit_bytes=limit),
        cost_estimate=pl.CostEstimate(flops=flops, bytes_accessed=4 * 1024 * 1024, transcendentals=0),
    )(*args)


def kernels(block, slab, channels):
    local_len, groups = block * slab, block // slab
    bf16, f32 = jnp.bfloat16, jnp.float32
    ANY, VMEM = pl.ANY, pltpu.VMEM
    message = jax.ShapeDtypeStruct((groups, 2 * slab * slab, channels), bf16)
    flat = jax.ShapeDtypeStruct((slab, block, channels), bf16)
    stage = VMEM((2, local_len, channels), f32)
    buffer = VMEM(message.shape, bf16)
    piece, matrix = VMEM((local_len, channels), bf16), VMEM((block, block), bf16)
    flops = 2 * block * block * slab * channels
    before = functools.partial(
        call, functools.partial(before_kernel, slab), message, ANY, [ANY] * 4,
        [piece, piece, matrix, matrix, stage, buffer], 4 + 2 * HALVES, WHOLE_VMEM, 2 * flops, {},
    )
    between = functools.partial(
        call, functools.partial(between_kernel, slab), (message, jax.ShapeDtypeStruct((slab, block, channels), f32)),
        (ANY, VMEM), [VMEM, VMEM, VMEM, ANY],
        [piece, VMEM((local_len, channels), f32), stage, buffer], 1 + 2 * HALVES, MOST_VMEM, 4 * flops, {},
    )
    after = functools.partial(
        call, functools.partial(after_kernel, slab), (flat, flat), (ANY, ANY), [VMEM] * 3,
        [VMEM((2, slab, block, channels), bf16)], 2 * HALVES, MOST_VMEM, 2 * flops, {},
    )
    return before, between, after


def batch_sum(terms):
    inner, outer, channels = terms.shape
    quarter = channels // 4
    place = lax.axis_index("batch")
    core, side = lax.rem(place, 2), lax.div(place, 2)
    parts = terms.reshape(inner, outer, 2, 2, quarter)
    mine = lax.dynamic_index_in_dim(parts, core, 3, keepdims=False)
    other = lax.dynamic_index_in_dim(parts, 1 - core, 3, keepdims=False).astype(jnp.bfloat16)
    got = lax.ppermute(other, "batch", [(0, 1), (1, 0), (2, 3), (3, 2)])
    pair = mine + got.astype(jnp.float32)
    keep = lax.dynamic_index_in_dim(pair, side, 2, keepdims=False)
    give = lax.dynamic_index_in_dim(pair, 1 - side, 2, keepdims=False).astype(jnp.bfloat16)
    got = lax.ppermute(give, "batch", [(0, 2), (2, 0), (1, 3), (3, 1)])
    return (keep + got.astype(jnp.float32)).transpose(1, 0, 2)


def body(tokens, grad_out, kernel, mix_inner, mix_outer, unmix_outer, unmix_inner):
    local_len, channels = tokens.shape[1:]
    block = mix_inner.shape[0]
    slab = local_len // block
    before, between, after = kernels(block, slab, channels)
    sent = before(tokens.reshape(local_len, channels), grad_out.reshape(local_len, channels), mix_inner, unmix_inner)
    here = lax.all_to_all(sent, "seq", split_axis=0, concat_axis=0, tiled=True)
    sent, terms = between(here, mix_outer, unmix_outer, kernel.reshape(local_len, channels))
    back = lax.all_to_all(sent, "seq", split_axis=0, concat_axis=0, tiled=True)
    grad_kernel = batch_sum(terms)
    output, grad_tokens = after(back, unmix_inner, mix_inner)
    return (output.reshape(1, local_len, channels), grad_tokens.reshape(1, local_len, channels), grad_kernel)


def solution(mesh):
    return jax.shard_map(
        body,
        mesh=mesh,
        in_specs=(
            P("batch", "seq", None),
            P("batch", "seq", None),
            P(None, "seq", None),
            P(),
            P(),
            P(),
            P(),
        ),
        out_specs=(P("batch", "seq", None), P("batch", "seq", None), P(None, "seq", "batch")),
        check_vma=False,
    )
```

```python
import functools

import jax
import jax.numpy as jnp
from jax import lax
from jax.experimental import pallas as pl
from jax.experimental.pallas import tpu as pltpu
from jax.sharding import PartitionSpec as P

SUBLANES = 8
HALVES = 2
WHOLE_VMEM = 62 * 1024 * 1024
MOST_VMEM = 24 * 1024 * 1024


def dot(left, right, left_dim=1):
    return lax.dot_general(left, right, (((left_dim,), (0,)), ((), ())), preferred_element_type=jnp.float32)


class Copies:
    def __init__(self, sems):
        self.sems, self.started = sems, []

    def start(self, src, dst):
        copy = pltpu.make_async_copy(src, dst, self.sems.at[len(self.started)])
        copy.start()
        self.started.append(copy)
        return copy


def halves(block):
    return [slice(h * (block // HALVES), (h + 1) * (block // HALVES)) for h in range(HALVES)]


def rows_of(weight, left_dim, cut):
    return weight[:, cut] if left_dim == 0 else weight[cut, :]


def send_product(slab, weight, left_dim, right, stage, out_buf, out_ref, part, copies):
    block, width = right.shape
    channels = width // slab
    rows = slab * slab
    here = pl.ds(part * rows, rows)
    given = []
    for cut in halves(block):
        product = dot(rows_of(weight, left_dim, cut), right, left_dim)
        height = cut.stop - cut.start
        for g in range(slab):
            stage[pl.ds(cut.start * slab + g, height, stride=slab), :] = product[:, g * channels : (g + 1) * channels]
        groups = pl.ds(cut.start // slab, height // slab)
        ready = stage[pl.ds(cut.start * slab, height * slab), :].astype(jnp.bfloat16)
        out_buf[groups, here, :] = ready.reshape(height // slab, rows, channels)
        given.append(copies.start(out_buf.at[groups, here], out_ref.at[groups, here]))
    return given


def gather_rows(slab, in_ref, part):
    groups, _, channels = in_ref.shape
    rows = slab * slab
    tiles = rows // SUBLANES
    got = in_ref[:, part * rows : (part + 1) * rows, :].astype(jnp.float32)
    got = got.reshape(groups // 2, 2, tiles, SUBLANES, channels)
    turned = pltpu.roll(got.reshape(groups * tiles, SUBLANES, channels), slab, axis=1).reshape(got.shape)
    low = lax.broadcasted_iota(jnp.int32, (groups // 2, tiles, SUBLANES, channels), 2) < slab
    even = jnp.where(low, got[:, 0], turned[:, 1]).astype(jnp.bfloat16)
    odd = jnp.where(low, turned[:, 0], got[:, 1]).astype(jnp.bfloat16)
    lanes = [half[:, t].reshape(groups * slab, channels) for t in range(tiles) for half in (even, odd)]
    return jnp.concatenate(lanes, axis=1)


def lanes_of(ref, slab):
    block = ref.shape[0] // slab
    return jnp.concatenate([ref[a * block : (a + 1) * block, :] for a in range(slab)], axis=1)


def before_kernel(slab, tok_hbm, cot_hbm, mix_hbm, unmix_hbm, out_ref, tok, cot, mix, unmix, stage, out_buf, sems):
    copies = Copies(sems)
    got = [copies.start(src, dst) for src, dst in ((mix_hbm, mix), (tok_hbm, tok), (unmix_hbm, unmix), (cot_hbm, cot))]
    given = []
    for part, (weight, data, left_dim) in enumerate(((mix, tok, 0), (unmix, cot, 1))):
        got[2 * part].wait()
        got[2 * part + 1].wait()
        given += send_product(slab, weight, left_dim, lanes_of(data, slab), stage.at[part], out_buf, out_ref, part, copies)
    for copy in given:
        copy.wait()


def between_kernel(slab, in_ref, mix, unmix, ker_hbm, out_ref, term_ref, ker, ker_rows, stage, out_buf, sems):
    block, channels = mix.shape[0], in_ref.shape[2]
    copies = Copies(sems)
    got_ker = copies.start(ker_hbm, ker)
    spectrum = dot(mix[...], gather_rows(slab, in_ref, 0), 0).astype(jnp.bfloat16).astype(jnp.float32)
    gradf = dot(unmix[...], gather_rows(slab, in_ref, 1)).astype(jnp.bfloat16).astype(jnp.float32)
    got_ker.wait()
    ker_rows[...] = ker[...].astype(jnp.float32)
    weight = jnp.concatenate([ker_rows[pl.ds(i, block, stride=slab), :] for i in range(slab)], axis=1)
    filtered = (weight * spectrum).astype(jnp.bfloat16)
    given = send_product(slab, unmix, 0, filtered, stage.at[0], out_buf, out_ref, 0, copies)
    grad_spectrum = (weight * gradf).astype(jnp.bfloat16)
    given += send_product(slab, mix, 1, grad_spectrum, stage.at[1], out_buf, out_ref, 1, copies)
    terms = spectrum * gradf
    for i in range(slab):
        term_ref[i] = terms[:, i * channels : (i + 1) * channels]
    for copy in given:
        copy.wait()


def after_kernel(slab, in_ref, unmix, mix, res_ref, tok_ref, out_buf, sems):
    channels = in_ref.shape[2]
    block = unmix.shape[0]
    copies = Copies(sems)
    given = []
    for part, (weight, left_dim, out_ref) in enumerate(((unmix, 0, res_ref), (mix, 1, tok_ref))):
        arrived = gather_rows(slab, in_ref, part)
        for cut in halves(block):
            product = dot(rows_of(weight, left_dim, cut), arrived, left_dim).astype(jnp.bfloat16)
            here = pl.ds(cut.start, cut.stop - cut.start)
            for i in range(slab):
                out_buf[part, i, here, :] = product[:, i * channels : (i + 1) * channels]
            given.append(copies.start(out_buf.at[part, :, here], out_ref.at[:, here]))
    for copy in given:
        copy.wait()


def call(kernel, outs, out_specs, specs, scratch, copies, limit, flops, aliases, *args):
    return pl.pallas_call(
        kernel,
        out_shape=outs,
        in_specs=[pl.BlockSpec(memory_space=space) for space in specs],
        out_specs=jax.tree.map(lambda space: pl.BlockSpec(memory_space=space), out_specs),
        scratch_shapes=[*scratch, pltpu.SemaphoreType.DMA((copies,))],
        input_output_aliases=aliases,
        compiler_params=pltpu.CompilerParams(vmem_limit_bytes=limit),
        cost_estimate=pl.CostEstimate(flops=flops, bytes_accessed=4 * 1024 * 1024, transcendentals=0),
    )(*args)


def kernels(block, slab, channels):
    local_len, groups = block * slab, block // slab
    bf16, f32 = jnp.bfloat16, jnp.float32
    ANY, VMEM = pl.ANY, pltpu.VMEM
    message = jax.ShapeDtypeStruct((groups, 2 * slab * slab, channels), bf16)
    flat = jax.ShapeDtypeStruct((slab, block, channels), bf16)
    stage = VMEM((2, local_len, channels), f32)
    buffer = VMEM(message.shape, bf16)
    piece, matrix = VMEM((local_len, channels), bf16), VMEM((block, block), bf16)
    flops = 2 * block * block * slab * channels
    before = functools.partial(
        call, functools.partial(before_kernel, slab), message, ANY, [ANY] * 4,
        [piece, piece, matrix, matrix, stage, buffer], 4 + 2 * HALVES, WHOLE_VMEM, 2 * flops, {},
    )
    between = functools.partial(
        call, functools.partial(between_kernel, slab), (message, jax.ShapeDtypeStruct((slab, block, channels), f32)),
        (ANY, VMEM), [VMEM, VMEM, VMEM, ANY],
        [piece, VMEM((local_len, channels), f32), stage, buffer], 1 + 2 * HALVES, MOST_VMEM, 4 * flops, {},
    )
    after = functools.partial(
        call, functools.partial(after_kernel, slab), (flat, flat), (ANY, ANY), [VMEM] * 3,
        [VMEM((2, slab, block, channels), bf16)], 2 * HALVES, MOST_VMEM, 2 * flops, {},
    )
    return before, between, after


def batch_sum(terms):
    inner, outer, channels = terms.shape
    quarter = channels // 4
    place = lax.axis_index("batch")
    core, side = lax.rem(place, 2), lax.div(place, 2)
    parts = terms.reshape(inner, outer, 2, 2, quarter)
    mine = lax.dynamic_index_in_dim(parts, core, 3, keepdims=False)
    other = lax.dynamic_index_in_dim(parts, 1 - core, 3, keepdims=False)
    pair = mine + lax.ppermute(other, "batch", [(0, 1), (1, 0), (2, 3), (3, 2)])
    keep = lax.dynamic_index_in_dim(pair, side, 2, keepdims=False)
    give = lax.dynamic_index_in_dim(pair, 1 - side, 2, keepdims=False)
    total = keep + lax.ppermute(give, "batch", [(0, 2), (2, 0), (1, 3), (3, 1)])
    return total.transpose(1, 0, 2)


def kernels(block, slab, channels):
    local_len, groups = block * slab, block // slab
    bf16, f32 = jnp.bfloat16, jnp.float32
    ANY, VMEM = pl.ANY, pltpu.VMEM
    message = jax.ShapeDtypeStruct((groups, 2 * slab * slab, channels), bf16)
    flat = jax.ShapeDtypeStruct((slab, block, channels), bf16)
    stage = VMEM((2, local_len, channels), f32)
    buffer = VMEM(message.shape, bf16)
    piece, matrix = VMEM((local_len, channels), bf16), VMEM((block, block), bf16)
    flops = 2 * block * block * slab * channels
    before = functools.partial(
        call, functools.partial(before_kernel, slab), message, ANY, [ANY] * 4,
        [piece, piece, matrix, matrix, stage, buffer], 4 + 2 * HALVES, WHOLE_VMEM, 2 * flops, {},
    )
    between = functools.partial(
        call, functools.partial(between_kernel, slab), (message, jax.ShapeDtypeStruct((slab, block, channels), f32)),
        (ANY, VMEM), [VMEM, VMEM, VMEM, ANY],
        [piece, VMEM((local_len, channels), f32), stage, buffer], 1 + 2 * HALVES, MOST_VMEM, 4 * flops, {},
    )
    after = functools.partial(
        call, functools.partial(after_kernel, slab), (flat, flat), (ANY, ANY), [VMEM] * 3,
        [VMEM((2, slab, block, channels), bf16)], 2 * HALVES, MOST_VMEM, 2 * flops, {},
    )
    return before, between, after


def batch_sum(terms):
    inner, outer, channels = terms.shape
    quarter = channels // 4
    place = lax.axis_index("batch")
    core, side = lax.rem(place, 2), lax.div(place, 2)
    parts = terms.reshape(inner, outer, 2, 2, quarter)
    mine = lax.dynamic_index_in_dim(parts, core, 3, keepdims=False)
    other = lax.dynamic_index_in_dim(parts, 1 - core, 3, keepdims=False).astype(jnp.bfloat16)
    got = lax.ppermute(other, "batch", [(0, 1), (1, 0), (2, 3), (3, 2)])
    pair = mine + got.astype(jnp.float32)
    keep = lax.dynamic_index_in_dim(pair, side, 2, keepdims=False)
    give = lax.dynamic_index_in_dim(pair, 1 - side, 2, keepdims=False).astype(jnp.bfloat16)
    got = lax.ppermute(give, "batch", [(0, 2), (2, 0), (1, 3), (3, 1)])
    return (keep + got.astype(jnp.float32)).transpose(1, 0, 2)


def body(tokens, grad_out, kernel, mix_inner, mix_outer, unmix_outer, unmix_inner):
    local_len, channels = tokens.shape[1:]
    block = mix_inner.shape[0]
    slab = local_len // block
    before, between, after = kernels(block, slab, channels)
    sent = before(tokens.reshape(local_len, channels), grad_out.reshape(local_len, channels), mix_inner, unmix_inner)
    here = lax.all_to_all(sent, "seq", split_axis=0, concat_axis=0, tiled=True)
    sent, terms = between(here, mix_outer, unmix_outer, kernel.reshape(local_len, channels))
    back = lax.all_to_all(sent, "seq", split_axis=0, concat_axis=0, tiled=True)
    grad_kernel = batch_sum(terms)
    output, grad_tokens = after(back, unmix_inner, mix_inner)
    return (output.reshape(1, local_len, channels), grad_tokens.reshape(1, local_len, channels), grad_kernel)


def solution(mesh):
    return jax.shard_map(
        body,
        mesh=mesh,
        in_specs=(
            P("batch", "seq", None),
            P("batch", "seq", None),
            P(None, "seq", None),
            P(),
            P(),
            P(),
            P(),
        ),
        out_specs=(P("batch", "seq", None), P("batch", "seq", None), P(None, "seq", "batch")),
        check_vma=False,
    )
```

```python
import functools

import jax
import jax.numpy as jnp
from jax import lax
from jax.experimental import pallas as pl
from jax.experimental.pallas import tpu as pltpu
from jax.sharding import PartitionSpec as P

SUBLANES = 8
HALVES = 2
WHOLE_VMEM = 62 * 1024 * 1024
MOST_VMEM = 24 * 1024 * 1024


def dot(left, right, left_dim=1):
    return lax.dot_general(left, right, (((left_dim,), (0,)), ((), ())), preferred_element_type=jnp.float32)


class Copies:
    def __init__(self, sems):
        self.sems, self.started = sems, []

    def start(self, src, dst):
        copy = pltpu.make_async_copy(src, dst, self.sems.at[len(self.started)])
        copy.start()
        self.started.append(copy)
        return copy


def halves(block):
    return [slice(h * (block // HALVES), (h + 1) * (block // HALVES)) for h in range(HALVES)]


def rows_of(weight, left_dim, cut):
    return weight[:, cut] if left_dim == 0 else weight[cut, :]


def send_product(slab, weight, left_dim, right, stage, out_buf, out_ref, part, copies):
    block, width = right.shape
    channels = width // slab
    rows = slab * slab
    here = pl.ds(part * rows, rows)
    given = []
    for cut in halves(block):
        product = dot(rows_of(weight, left_dim, cut), right, left_dim)
        height = cut.stop - cut.start
        for g in range(slab):
            stage[pl.ds(cut.start * slab + g, height, stride=slab), :] = product[:, g * channels : (g + 1) * channels]
        groups = pl.ds(cut.start // slab, height // slab)
        ready = stage[pl.ds(cut.start * slab, height * slab), :].astype(jnp.bfloat16)
        out_buf[groups, here, :] = ready.reshape(height // slab, rows, channels)
        given.append(copies.start(out_buf.at[groups, here], out_ref.at[groups, here]))
    return given


def gather_rows(slab, in_ref, part):
    groups, _, channels = in_ref.shape
    rows = slab * slab
    tiles = rows // SUBLANES
    got = in_ref[:, part * rows : (part + 1) * rows, :].astype(jnp.float32)
    got = got.reshape(groups // 2, 2, tiles, SUBLANES, channels)
    turned = pltpu.roll(got.reshape(groups * tiles, SUBLANES, channels), slab, axis=1).reshape(got.shape)
    low = lax.broadcasted_iota(jnp.int32, (groups // 2, tiles, SUBLANES, channels), 2) < slab
    even = jnp.where(low, got[:, 0], turned[:, 1]).astype(jnp.bfloat16)
    odd = jnp.where(low, turned[:, 0], got[:, 1]).astype(jnp.bfloat16)
    lanes = [half[:, t].reshape(groups * slab, channels) for t in range(tiles) for half in (even, odd)]
    return jnp.concatenate(lanes, axis=1)


def lanes_of(ref, slab):
    block = ref.shape[0] // slab
    return jnp.concatenate([ref[a * block : (a + 1) * block, :] for a in range(slab)], axis=1)


def before_kernel(slab, tok_hbm, cot_hbm, mix_hbm, unmix_hbm, out_ref, tok, cot, mix, unmix, stage, out_buf, sems):
    copies = Copies(sems)
    got = [copies.start(src, dst) for src, dst in ((mix_hbm, mix), (tok_hbm, tok), (unmix_hbm, unmix), (cot_hbm, cot))]
    given = []
    for part, (weight, data, left_dim) in enumerate(((mix, tok, 0), (unmix, cot, 1))):
        got[2 * part].wait()
        got[2 * part + 1].wait()
        given += send_product(slab, weight, left_dim, lanes_of(data, slab), stage.at[part], out_buf, out_ref, part, copies)
    for copy in given:
        copy.wait()


def between_kernel(slab, in_ref, mix, unmix, ker_hbm, out_ref, term_ref, ker, ker_rows, stage, out_buf, sems):
    block, channels = mix.shape[0], in_ref.shape[2]
    copies = Copies(sems)
    got_ker = copies.start(ker_hbm, ker)
    spectrum = dot(mix[...], gather_rows(slab, in_ref, 0), 0).astype(jnp.bfloat16).astype(jnp.float32)
    gradf = dot(unmix[...], gather_rows(slab, in_ref, 1)).astype(jnp.bfloat16).astype(jnp.float32)
    got_ker.wait()
    ker_rows[...] = ker[...].astype(jnp.float32)
    weight = jnp.concatenate([ker_rows[pl.ds(i, block, stride=slab), :] for i in range(slab)], axis=1)
    filtered = (weight * spectrum).astype(jnp.bfloat16)
    given = send_product(slab, unmix, 0, filtered, stage.at[0], out_buf, out_ref, 0, copies)
    grad_spectrum = (weight * gradf).astype(jnp.bfloat16)
    given += send_product(slab, mix, 1, grad_spectrum, stage.at[1], out_buf, out_ref, 1, copies)
    terms = spectrum * gradf
    for i in range(slab):
        term_ref[i] = terms[:, i * channels : (i + 1) * channels]
    for copy in given:
        copy.wait()


def after_kernel(slab, in_ref, unmix, mix, res_ref, tok_ref, out_buf, sems):
    channels = in_ref.shape[2]
    block = unmix.shape[0]
    copies = Copies(sems)
    given = []
    for part, (weight, left_dim, out_ref) in enumerate(((unmix, 0, res_ref), (mix, 1, tok_ref))):
        arrived = gather_rows(slab, in_ref, part)
        for cut in halves(block):
            product = dot(rows_of(weight, left_dim, cut), arrived, left_dim).astype(jnp.bfloat16)
            here = pl.ds(cut.start, cut.stop - cut.start)
            for i in range(slab):
                out_buf[part, i, here, :] = product[:, i * channels : (i + 1) * channels]
            given.append(copies.start(out_buf.at[part, :, here], out_ref.at[:, here]))
    for copy in given:
        copy.wait()


def call(kernel, outs, out_specs, specs, scratch, copies, limit, flops, aliases, *args):
    return pl.pallas_call(
        kernel,
        out_shape=outs,
        in_specs=[pl.BlockSpec(memory_space=space) for space in specs],
        out_specs=jax.tree.map(lambda space: pl.BlockSpec(memory_space=space), out_specs),
        scratch_shapes=[*scratch, pltpu.SemaphoreType.DMA((copies,))],
        input_output_aliases=aliases,
        compiler_params=pltpu.CompilerParams(vmem_limit_bytes=limit),
        cost_estimate=pl.CostEstimate(flops=flops, bytes_accessed=4 * 1024 * 1024, transcendentals=0),
    )(*args)


def kernels(block, slab, channels):
    local_len, groups = block * slab, block // slab
    bf16, f32 = jnp.bfloat16, jnp.float32
    ANY, VMEM = pl.ANY, pltpu.VMEM
    message = jax.ShapeDtypeStruct((groups, 2 * slab * slab, channels), bf16)
    flat = jax.ShapeDtypeStruct((slab, block, channels), bf16)
    stage = VMEM((2, local_len, channels), f32)
    buffer = VMEM(message.shape, bf16)
    piece, matrix = VMEM((local_len, channels), bf16), VMEM((block, block), bf16)
    flops = 2 * block * block * slab * channels
    before = functools.partial(
        call, functools.partial(before_kernel, slab), message, ANY, [ANY] * 4,
        [piece, piece, matrix, matrix, stage, buffer], 4 + 2 * HALVES, WHOLE_VMEM, 2 * flops, {},
    )
    between = functools.partial(
        call, functools.partial(between_kernel, slab), (message, jax.ShapeDtypeStruct((slab, block, channels), f32)),
        (ANY, VMEM), [VMEM, VMEM, VMEM, ANY],
        [piece, VMEM((local_len, channels), f32), stage, buffer], 1 + 2 * HALVES, MOST_VMEM, 4 * flops, {},
    )
    after = functools.partial(
        call, functools.partial(after_kernel, slab), (flat, flat), (ANY, ANY), [VMEM] * 3,
        [VMEM((2, slab, block, channels), bf16)], 2 * HALVES, MOST_VMEM, 2 * flops, {},
    )
    return before, between, after


def batch_sum(terms):
    inner, outer, channels = terms.shape
    quarter = channels // 4
    place = lax.axis_index("batch")
    core, side = lax.rem(place, 2), lax.div(place, 2)
    parts = terms.reshape(inner, outer, 2, 2, quarter)
    mine = lax.dynamic_index_in_dim(parts, core, 3, keepdims=False)
    other = lax.dynamic_index_in_dim(parts, 1 - core, 3, keepdims=False)
    pair = mine + lax.ppermute(other, "batch", [(0, 1), (1, 0), (2, 3), (3, 2)])
    keep = lax.dynamic_index_in_dim(pair, side, 2, keepdims=False)
    give = lax.dynamic_index_in_dim(pair, 1 - side, 2, keepdims=False)
    total = keep + lax.ppermute(give, "batch", [(0, 2), (2, 0), (1, 3), (3, 1)])
    return total.transpose(1, 0, 2)


def body(tokens, grad_out, kernel, mix_inner, mix_outer, unmix_outer, unmix_inner):
    local_len, channels = tokens.shape[1:]
    block = mix_inner.shape[0]
    slab = local_len // block
    before, between, after = kernels(block, slab, channels)
    sent = before(tokens.reshape(local_len, channels), grad_out.reshape(local_len, channels), mix_inner, unmix_inner)
    here = lax.all_to_all(sent, "seq", split_axis=0, concat_axis=0, tiled=True)
    sent, terms = between(here, mix_outer, unmix_outer, kernel.reshape(local_len, channels))
    back = lax.all_to_all(sent, "seq", split_axis=0, concat_axis=0, tiled=True)
    grad_kernel = batch_sum(terms)
    output, grad_tokens = after(back, unmix_inner, mix_inner)
    return (output.reshape(1, local_len, channels), grad_tokens.reshape(1, local_len, channels), grad_kernel)


def solution(mesh):
    return jax.shard_map(
        body,
        mesh=mesh,
        in_specs=(
            P("batch", "seq", None),
            P("batch", "seq", None),
            P(None, "seq", None),
            P(),
            P(),
            P(),
            P(),
        ),
        out_specs=(P("batch", "seq", None), P("batch", "seq", None), P(None, "seq", "batch")),
        check_vma=False,
    )
```
